256 devices in a mesh: row: 8 (over x, y_lo), col: 32 (over z, y_hi, core).
Axes of the slice: x: 4, y: 4 (y_hi: 2, y_lo: 2; y = y_hi * 2 + y_lo), z: 8, core: 2. Of those that a mesh axis runs over, the one named last changes fastest.
Arguments:
- sigma: float32 [16384, 16384], P('col', 'row'), as said below
- factor: float32 [4096, 1024], P('row', 'col'), may hold values from -0.1875 to 0.1875
- blk_map: int32 [32], P('row'), may hold values from 0 to 127, as said below
- base_var: float32 [1024], P('col'), may hold values from 0.5 to 2
Outputs:
- cross: float32 [16384, 1024], P(('col', 'row'))
- variance: float32 [1024], P('col')
The draws below stay inside these ranges and needn't reach their ends.
Inputs may be any that keep to these rules, and one draw needn't show every extreme that they name: `blk_map`: entries r * 4 to r * 4 + 3 name distinct parent blocks of r * 16 to r * 16 + 15 in increasing order, the last block of that range always among them. `sigma`: symmetric.
All inputs are finite; a program needn't handle non-finite values.
Results may differ from the reference program's by a relative error of at most 0.000073.
Values sent between devices are 32-bit elements; how exact they have to be, the bound alone decides.
A program may use at most 64 MiB of HBM per device.

```python
import math
import jax
import jax.numpy as jnp
from jax import lax

P_SIZE = 16384
M = 4096
NC = 1024
BLK = 128
MB = 32
RB = 16
KB = 4
N_ROW = 8


def draw_sigma(key, part):
    key_off = jax.random.fold_in(key, 11)
    key_diag = jax.random.fold_in(key, 12)
    key_scale = jax.random.fold_in(key, 13)
    raw = jax.random.uniform(key_off, (P_SIZE, P_SIZE), jnp.float32, -1.0, 1.0)
    offdiag = (raw + raw.T) * (0.6 / P_SIZE ** 0.5)
    diag_vals = jax.random.uniform(key_diag, (P_SIZE,), jnp.float32, 1.0, 2.0)
    ids = jnp.arange(P_SIZE, dtype=jnp.int32)
    inner = jnp.where(ids[:, None] == ids[None, :], diag_vals[:, None], offdiag)
    trend = 1.0 + 2.0 * ids.astype(jnp.float32) / (P_SIZE - 1)
    rough = jnp.exp(jax.random.uniform(key_scale, (P_SIZE,), jnp.float32, -0.35, 0.35))
    scales = trend * rough
    return (scales[:, None] * inner * scales[None, :]).astype(jnp.float32)


def draw_blk_map(key, part):
    keys = jax.random.split(jax.random.fold_in(key, 21), N_ROW)

    def one_range(range_key):
        chosen = jax.random.permutation(range_key, RB - 1)[:KB - 1]
        ordered = jnp.sort(chosen.astype(jnp.int32))
        return jnp.concatenate([ordered, jnp.full((1,), RB - 1, jnp.int32)])
    blocks = jax.vmap(one_range)(keys)
    bases = (jnp.arange(N_ROW, dtype=jnp.int32) * RB)[:, None]
    return (blocks + bases).reshape(MB).astype(jnp.int32)


def block_levels(rng, shape, cuts, smallest, top_value):
    loudness = 1.0
    for axis_at, shards_of in cuts:
        heights = jax.random.uniform(jax.random.fold_in(jax.random.fold_in(rng, 6), axis_at), (shards_of,), jnp.float32, smallest / len(cuts), top_value / len(cuts))
        loudness = loudness * jnp.repeat(jnp.exp(heights), shape[axis_at] // shards_of).reshape((-1,) + (1,) * (len(shape) - 1 - axis_at))
    return loudness


def noise(stream_key, shape, deviation, bound, cuts=(), kind=jnp.bfloat16):
    loudness = block_levels(stream_key, shape, cuts, -0.22, 0.18) if cuts else 1.0
    entries = jax.random.normal(stream_key, shape, jnp.float32) * deviation * loudness
    return jnp.minimum(jnp.maximum(entries, -bound), bound).astype(kind)


def setup_inputs(seed: int = 0) -> dict:
    key_of = jax.random.split(jax.random.key(seed), 5)
    return {
        "sigma": draw_sigma(jax.random.fold_in(key_of[4], 71), 0),
        "factor": noise(key_of[1], (M, NC), (2.0 / M ** 0.5), 0.1875, ((0, 8), (1, 32)), jnp.float32),
        "blk_map": draw_blk_map(jax.random.fold_in(key_of[4], 71), 0),
        "base_var": jnp.clip(jnp.exp(math.log(2.0) - 1.3862944 * jax.random.uniform(key_of[3], (NC,), jnp.float32) ** block_levels(key_of[3], (NC,), ((0, 32),), -0.2, 0.2)), 0.5, 2.0),
    }


def reference(sigma, factor, blk_map, base_var):
    child = jnp.arange(M, dtype=jnp.int32)
    prow = (blk_map[child // BLK] * BLK + child % BLK).astype(jnp.int32)
    picked = jnp.take(sigma, prow, axis=1)
    panel = jnp.dot(picked, factor, precision=lax.Precision.HIGHEST, preferred_element_type=jnp.float32)
    cross = -panel
    variance = base_var + jnp.sum(factor * jnp.take(panel, prow, axis=0), axis=0)
    return cross, variance
```

```python
import functools

import jax
import jax.numpy as jnp
from jax import lax
from jax.experimental import pallas as pl
from jax.experimental.pallas import tpu as pltpu
from jax.sharding import PartitionSpec as P

MESH = pl.DeviceIdType.MESH
BLK = 128
POS = {0: 0, 4: 1, 1: 2, 7: 3, 2: 4, 6: 5, 3: 6, 5: 7}
XFIRST = (1, 2, 3, 0)


def kernel(
    sig_hbm, fact_ref, blk_ref, base_ref, out_ref, var_ref,
    sig, acat, front, part, xr, yr, stage, ls_src, ls1, lift, sv, va, vb_src, vb,
    sig_sem, agz_s, agz_r, yh_s, yh_r, sib_s, sib_r, l1_s, l1_r, l2_s, l2_r,
    x_s, x_r, y_s, y_r, va_s, va_r, vb_s, vb_r,
):
    r = lax.axis_index("row")
    c = lax.axis_index("col")
    x, yl = r // 2, r % 2
    z, yh, co = c // 4, (c // 2) % 2, c % 2
    k = c % 4

    def dev(dx=0, dy=0, dz=0, dh=0, dc=0):
        return (
            ((x + dx) % 4) * 2 + (yl + dy) % 2,
            ((z + dz) % 8) * 4 + ((yh + dh) % 2) * 2 + (co + dc) % 2,
        )

    def send(src, dst, ssem, rsem, to):
        cp = pltpu.make_async_remote_copy(
            src, dst, ssem, rsem, device_id=to, device_id_type=MESH
        )
        cp.start()
        return cp

    pending = []

    def push(*args):
        cp = send(*args)
        pending.append(cp)
        return cp

    cp_sig = pltpu.make_async_copy(sig_hbm, sig, sig_sem)
    cp_sig.start()
    plane = [
        (dx, dy, dh, dc)
        for dx in range(4) for dy in range(2) for dh in range(2) for dc in range(2)
    ][1:]
    barrier = pltpu.get_barrier_semaphore()
    for dx, dy, dh, dc in plane:
        pl.semaphore_signal(barrier, inc=1, device_id=dev(dx, dy, 0, dh, dc), device_id_type=MESH)
    for dz in range(1, 8):
        pl.semaphore_signal(barrier, inc=1, device_id=dev(dz=dz), device_id_type=MESH)

    def rows(op):
        src_k = k if op == 0 else ((yh + 1) % 2) * 2 + co
        return pl.ds(pl.multiple_of(src_k * 32, 32), 32)

    def piece(d, op):
        return front.at[POS[d], rows(op)]

    front[POS[0], rows(0), :] = fact_ref[...]
    cp_sig.wait()
    def pick(step, carry):
        at = pl.ds(pl.multiple_of(step * 32, 32), 32)
        for i in range(4):
            if i == 3:
                a = sig[at, 15 * BLK:16 * BLK]
            else:
                where = jnp.full((32, BLK), blk_ref[i] - r * 16, jnp.int32)
                a = sig[at, i * BLK:(i + 1) * BLK]
                for b in range(i + 1, i + 13):
                    a = jnp.where(where == b, sig[at, b * BLK:(b + 1) * BLK], a)
            hi = a.astype(jnp.bfloat16)
            lo = (a - hi.astype(jnp.float32)).astype(jnp.bfloat16)
            acat[at, i * BLK:(i + 1) * BLK] = hi
            acat[at, 512 + i * BLK:512 + (i + 1) * BLK] = hi
            acat[at, 1024 + i * BLK:1024 + (i + 1) * BLK] = lo
        return carry

    lax.fori_loop(0, 16, pick, 0)

    pl.semaphore_wait(barrier, len(plane) + 7)

    zcp = {}

    def zsend(d, op):
        for side, (dz, nd) in enumerate(((1, d + 1), (-1, (d - 1) % 8))):
            if d != 0 and (side == 0) != (d < 4):
                continue
            if nd == 4 and op != side:
                continue
            slot = nd * 2 + op
            zcp[nd, op] = push(piece(d, op), piece(nd, op), agz_s.at[slot], agz_r.at[slot], dev(dz=dz))

    sibcp = {}

    def sibsend(d, op):
        slot = d * 2 + op
        sibcp[d, op] = push(piece(d, op), piece(d, op), sib_s.at[slot], sib_r.at[slot], dev(dc=1))

    def arrive(d, op):
        zcp[d, op].wait_recv()
        if d != 4:
            zsend(d, op)
        sibsend(d, op)

    zsend(0, 0)
    cp_yh = push(front.at[POS[0], rows(0)], front.at[POS[0], rows(0)], yh_s, yh_r, dev(dh=1))
    sibsend(0, 0)
    arrive(1, 0)
    arrive(7, 0)
    cp_yh.wait_recv()
    zsend(0, 1)
    sibsend(0, 1)

    def sibwait(d):
        sibcp[d, 0].wait_recv()
        sibcp[d, 1].wait_recv()

    sibwait(0)
    ft = [front[POS[0], :, i * BLK:(i + 1) * BLK].T for i in range(4)]
    for b in range(4):
        blk = jnp.zeros((BLK, BLK), jnp.float32)
        for i in range(4):
            where = jnp.full((BLK, BLK), blk_ref[i] - r * 16, jnp.int32)
            blk = jnp.where(where == k * 4 + b, ft[i], blk)
        ls_src[2 * b] = blk[:64]
        ls_src[2 * b + 1] = blk[64:]
    l1 = []
    for dx in range(4):
        for dy in range(2):
            if dx + dy == 0:
                continue
            i = dx * 2 + dy
            to = dev(dx, dy)
            l1.append(push(ls_src.at[to[0]], ls1.at[r], l1_s.at[i], l1_r.at[i], to))
    ls1[r] = ls_src[r]

    cps = {}

    def rs_start(ds):
        n = len(ds)
        f = front[POS[ds[0]]:POS[ds[0]] + n].reshape(n * BLK, 512)
        hi = f.astype(jnp.bfloat16)
        lo = (f - hi.astype(jnp.float32)).astype(jnp.bfloat16)
        fcat = jnp.concatenate([hi, lo, hi], axis=1)
        res = lax.dot_general(
            acat[...], fcat, (((1,), (1,)), ((), ())), preferred_element_type=jnp.float32
        )
        for m, d in enumerate(ds):
            part[d] = res[:, m * BLK:(m + 1) * BLK].reshape(4, 2, 64, BLK)
        for d in ds:
            if d in XFIRST:
                for dx in range(1, 4):
                    cps[d, "x", dx] = push(
                        part.at[d, (x + dx) % 4], xr.at[d, dx - 1],
                        x_s.at[d * 3 + dx - 1], x_r.at[d * 3 + dx - 1], dev(dx=dx))
            else:
                cps[d, "y"] = push(part.at[d, :, 1 - yl], yr.at[d], y_s.at[d], y_r.at[d], dev(dy=1))

    def rs_mid(d):
        if d in XFIRST:
            for dx in range(1, 4):
                cps[d, "x", dx].wait_recv()
            stage[d, 0:2] = part[d, x] + xr[d, 0] + xr[d, 1] + xr[d, 2]
            cps[d, "y"] = push(stage.at[d, 1 - yl], yr.at[d, 0], y_s.at[d], y_r.at[d], dev(dy=1))
        else:
            cps[d, "y"].wait_recv()
            stage[d] = part[d, :, yl] + yr[d]
            for dx in range(1, 4):
                cps[d, "x", dx] = push(
                    stage.at[d, (x + dx) % 4], xr.at[d, dx - 1, 0],
                    x_s.at[d * 3 + dx - 1], x_r.at[d * 3 + dx - 1], dev(dx=dx))

    vacp = {}

    def rs_end(d):
        if d in XFIRST:
            cps[d, "y"].wait_recv()
            panel = stage[d, yl] + yr[d, 0]
        else:
            for dx in range(1, 4):
                cps[d, "x", dx].wait_recv()
            panel = stage[d, x] + xr[d, 0, 0] + xr[d, 1, 0] + xr[d, 2, 0]
        j = (z - d) % 8
        out_ref[:, pl.ds(pl.multiple_of(j * BLK, BLK), BLK)] = panel
        if d:
            l2cp[d].wait_recv()
        s = jnp.sum((panel * lift[d]).reshape(8, 8, BLK), axis=0)
        if d:
            sv[d] = s
            vacp[d] = push(sv.at[d], va.at[d], va_s.at[d], va_r.at[d], dev(dz=-d))
        else:
            va[0] = s

    arrive(2, 0)
    arrive(6, 0)
    arrive(1, 1)
    arrive(7, 1)
    sibwait(1)
    sibwait(7)
    rs_start((1, 7))
    arrive(3, 0)
    arrive(5, 0)
    arrive(2, 1)
    arrive(6, 1)
    sibwait(2)
    sibwait(6)
    rs_start((2, 6))
    for cp in l1:
        cp.wait_recv()
    l2cp = {}
    for dz in range(1, 8):
        l2cp[dz] = push(ls1.at[(z + dz) % 8], lift.at[dz], l2_s.at[dz], l2_r.at[dz], dev(dz=dz))
    lift[0] = ls1[z]
    rs_mid(1)
    rs_mid(7)
    arrive(4, 0)
    arrive(3, 1)
    arrive(5, 1)
    sibwait(3)
    sibwait(5)
    rs_start((3, 5))
    rs_mid(2)
    rs_mid(6)
    rs_end(1)
    rs_end(7)
    arrive(4, 1)
    sibwait(4)
    rs_start((4,))
    rs_start((0,))
    rs_mid(3)
    rs_mid(5)
    rs_end(2)
    rs_end(6)
    rs_mid(4)
    rs_mid(0)
    rs_end(3)
    rs_end(5)
    rs_end(4)
    rs_end(0)

    for d in range(1, 8):
        vacp[d].wait_recv()
    total = va[0]
    for d in range(1, 8):
        total = total + va[d]
    vb_src[...] = total
    vbcp = []
    for i, (dx, dy, dh, dc) in enumerate(plane):
        vbcp.append(push(vb_src, vb.at[i], vb_s.at[i], vb_r.at[i], dev(dx, dy, 0, dh, dc)))
    for cp in vbcp:
        cp.wait_recv()
    total = jnp.sum(total + jnp.sum(vb[...], axis=0), axis=0, keepdims=True)
    own = total[:, 0:32]
    for kk in range(1, 4):
        own = jnp.where(k == kk, total[:, kk * 32:kk * 32 + 32], own)
    var_ref[...] = base_ref[...] + own
    for cp in pending:
        cp.wait_send()


def per_device(sigma, factor, blk_map, base_var):
    f32 = jnp.float32
    vm = lambda *s: pltpu.VMEM(s, f32)
    dma = lambda n: pltpu.SemaphoreType.DMA((n,))
    vmem = pl.BlockSpec(memory_space=pltpu.VMEM)
    panel, var = pl.pallas_call(
        kernel,
        out_shape=(jax.ShapeDtypeStruct((64, 1024), f32), jax.ShapeDtypeStruct((1, 32), f32)),
        in_specs=[
            pl.BlockSpec(memory_space=pl.ANY), vmem, pl.BlockSpec(memory_space=pltpu.SMEM), vmem,
        ],
        out_specs=(vmem, vmem),
        scratch_shapes=[
            vm(512, 2048), pltpu.VMEM((512, 1536), jnp.bfloat16), vm(8, 128, 512),
            vm(8, 4, 2, 64, 128), vm(8, 3, 2, 64, 128), vm(8, 4, 64, 128), vm(8, 4, 64, 128),
            vm(8, 64, 128), vm(8, 64, 128), vm(8, 64, 128),
            vm(8, 8, 128), vm(8, 8, 128), vm(8, 128), vm(31, 8, 128),
            pltpu.SemaphoreType.DMA,
            dma(16), dma(16), pltpu.SemaphoreType.DMA, pltpu.SemaphoreType.DMA, dma(16), dma(16),
            dma(8), dma(8), dma(8), dma(8),
            dma(24), dma(24), dma(8), dma(8), dma(8), dma(8), dma(31), dma(31),
        ],
        compiler_params=pltpu.CompilerParams(
            collective_id=0, has_side_effects=True, vmem_limit_bytes=56 * 2**20
        ),
    )(sigma, factor.T, blk_map, base_var.reshape(1, 32))
    return -panel, var.reshape(32)


def solution(mesh):
    return jax.shard_map(
        per_device,
        mesh=mesh,
        in_specs=(P("col", "row"), P("row", "col"), P("row"), P("col")),
        out_specs=(P(("col", "row"), None), P("col")),
        check_vma=False,
    )
```

```python
import functools

import jax
import jax.numpy as jnp
from jax import lax
from jax.experimental import pallas as pl
from jax.experimental.pallas import tpu as pltpu
from jax.sharding import PartitionSpec as P

MESH = pl.DeviceIdType.MESH
BLK = 128
POS = {0: 0, 4: 1, 1: 2, 7: 3, 2: 4, 6: 5, 3: 6, 5: 7}
XFIRST = (1, 2, 3)


def kernel(
    sig_hbm, fact_hbm, blk_ref, out_hbm, var_ref,
    pan, in_sem, out_sem,
    sig, acat, front, part, xr, yr, stage, ls_src, ls1, lift, sv, va, vb_src, vb,
    sig_sem, agz_s, agz_r, yh_s, yh_r, sib_s, sib_r, l1_s, l1_r, l2_s, l2_r,
    x_s, x_r, y_s, y_r, va_s, va_r, vb_s, vb_r, dr, d_s, d_r,
):
    r = lax.axis_index("row")
    c = lax.axis_index("col")
    x, yl = r // 2, r % 2
    z, yh, co = c // 4, (c // 2) % 2, c % 2
    k = c % 4

    def dev(dx=0, dy=0, dz=0, dh=0, dc=0):
        return (
            ((x + dx) % 4) * 2 + (yl + dy) % 2,
            ((z + dz) % 8) * 4 + ((yh + dh) % 2) * 2 + (co + dc) % 2,
        )

    def send(src, dst, ssem, rsem, to):
        cp = pltpu.make_async_remote_copy(
            src, dst, ssem, rsem, device_id=to, device_id_type=MESH
        )
        cp.start()
        return cp

    pending = []

    def push(*args):
        cp = send(*args)
        pending.append(cp)
        return cp

    everyone = [
        (dx, dy, dh, dc)
        for dx in range(4) for dy in range(2) for dh in range(2) for dc in range(2)
    ]
    plane = everyone[1:]
    barrier = pltpu.get_barrier_semaphore()
    peers = [dev(dx, dy) for dx in range(4) for dy in range(2)][1:]
    peers += [dev(dh=1), dev(dc=1)]
    peers += [dev(dz=dz, dh=dh) for dz in (1, -1) for dh in (0, 1)]
    for to in peers:
        pl.semaphore_signal(barrier, inc=1, device_id=to, device_id_type=MESH)

    def rows(op):
        src_k = k if op == 0 else ((yh + 1) % 2) * 2 + co
        return pl.ds(pl.multiple_of(src_k * 32, 32), 32)

    def piece(d, op):
        return front.at[POS[d], rows(op)]

    cp_fact = pltpu.make_async_copy(fact_hbm, piece(0, 0), in_sem.at[0])
    cp_fact.start()
    cp_sig = pltpu.make_async_copy(sig_hbm, sig, sig_sem)
    cp_sig.start()
    cp_sig.wait()
    def pick(step, carry):
        at = pl.ds(pl.multiple_of(step * 32, 32), 32)
        for i in range(4):
            if i == 3:
                a = sig[at, 15 * BLK:16 * BLK]
            else:
                where = jnp.full((32, BLK), blk_ref[i] - r * 16, jnp.int32)
                a = sig[at, i * BLK:(i + 1) * BLK]
                for b in range(i + 1, i + 13):
                    a = jnp.where(where == b, sig[at, b * BLK:(b + 1) * BLK], a)
            hi = a.astype(jnp.bfloat16)
            lo = (a - hi.astype(jnp.float32)).astype(jnp.bfloat16)
            acat[at, i * BLK:(i + 1) * BLK] = hi
            acat[at, 512 + i * BLK:512 + (i + 1) * BLK] = hi
            acat[at, 1024 + i * BLK:1024 + (i + 1) * BLK] = lo
        return carry

    lax.fori_loop(0, 16, pick, 0)

    pl.semaphore_wait(barrier, len(peers))

    zcp = {}

    def zsend(d, op):
        for side, (dz, nd) in enumerate(((1, d + 1), (-1, (d - 1) % 8))):
            if d != 0 and (side == 0) != (d < 4):
                continue
            if nd == 4 and op != side:
                continue
            slot = nd * 2 + op
            zcp[nd, op] = push(piece(d, op), piece(nd, op), agz_s.at[slot], agz_r.at[slot], dev(dz=dz))

    sibcp = {}

    def sibsend(d, op):
        slot = d * 2 + op
        sibcp[d, op] = push(piece(d, op), piece(d, op), sib_s.at[slot], sib_r.at[slot], dev(dc=1))

    def arrive(d, op):
        zcp[d, op].wait_recv()
        if d != 4:
            zsend(d, op)
        sibsend(d, op)

    cp_fact.wait()
    zsend(0, 0)
    own = piece(0, 0)
    for d, dz in ((1, 1), (7, -1)):
        slot = d * 2 + 1
        zcp[d, 1] = push(own, front.at[POS[d], rows(0)], agz_s.at[slot], agz_r.at[slot], dev(dz=dz, dh=1))
    cp_yh = push(own, own, yh_s, yh_r, dev(dh=1))
    sibsend(0, 0)
    arrive(1, 0)
    arrive(7, 0)
    cp_yh.wait_recv()
    sibsend(0, 1)

    def sibwait(d):
        sibcp[d, 0].wait_recv()
        sibcp[d, 1].wait_recv()

    l1 = []
    l2cp = {}

    def lift_start():
        ft = [front[POS[0], :, i * BLK:(i + 1) * BLK].T for i in range(4)]
        for b in range(4):
            blk = jnp.zeros((BLK, BLK), jnp.float32)
            for i in range(4):
                where = jnp.full((BLK, BLK), blk_ref[i] - r * 16, jnp.int32)
                blk = jnp.where(where == k * 4 + b, ft[i], blk)
            ls_src[2 * b] = blk[:64]
            ls_src[2 * b + 1] = blk[64:]
        for dx in range(4):
            for dy in range(2):
                if dx + dy == 0:
                    continue
                i = dx * 2 + dy
                to = dev(dx, dy)
                l1.append(push(ls_src.at[to[0]], ls1.at[r], l1_s.at[i], l1_r.at[i], to))
        ls1[r] = ls_src[r]

    cps = {}

    def rs_start(ds):
        n = len(ds)
        f = front[POS[ds[0]]:POS[ds[0]] + n].reshape(n * BLK, 512)
        hi = f.astype(jnp.bfloat16)
        lo = (f - hi.astype(jnp.float32)).astype(jnp.bfloat16)
        fcat = jnp.concatenate([hi, lo, hi], axis=1)
        res = lax.dot_general(
            acat[...], fcat, (((1,), (1,)), ((), ())), preferred_element_type=jnp.float32
        )
        for m, d in enumerate(ds):
            part[d] = res[:, m * BLK:(m + 1) * BLK].reshape(4, 2, 64, BLK)
        for d in ds:
            if d == 4:
                for dx in range(4):
                    for dy in range(2):
                        if dx + dy:
                            i = dx * 2 + dy - 1
                            to = dev(dx, dy)
                            cps[d, i] = push(part.at[d, to[0] // 2, to[0] % 2], dr.at[i], d_s.at[i], d_r.at[i], to)
            elif d in XFIRST:
                for dx in range(1, 4):
                    cps[d, "x", dx] = push(
                        part.at[d, (x + dx) % 4], xr.at[d, dx - 1],
                        x_s.at[d * 3 + dx - 1], x_r.at[d * 3 + dx - 1], dev(dx=dx))
            else:
                cps[d, "y"] = push(part.at[d, :, 1 - yl], yr.at[d], y_s.at[d], y_r.at[d], dev(dy=1))

    def rs_mid(d):
        if d in XFIRST:
            for dx in range(1, 4):
                cps[d, "x", dx].wait_recv()
            stage[d, 0:2] = part[d, x] + xr[d, 0] + xr[d, 1] + xr[d, 2]
            cps[d, "y"] = push(stage.at[d, 1 - yl], yr.at[d, 0], y_s.at[d], y_r.at[d], dev(dy=1))
        else:
            cps[d, "y"].wait_recv()
            stage[d] = part[d, :, yl] + yr[d]
            for dx in range(1, 4):
                cps[d, "x", dx] = push(
                    stage.at[d, (x + dx) % 4], xr.at[d, dx - 1, 0],
                    x_s.at[d * 3 + dx - 1], x_r.at[d * 3 + dx - 1], dev(dx=dx))

    vacp = {}
    outs = []

    def rs_end(d):
        if d == 4:
            panel = part[d, x, yl]
            for i in range(7):
                cps[d, i].wait_recv()
                panel = panel + dr[i]
        elif d in XFIRST:
            cps[d, "y"].wait_recv()
            panel = stage[d, yl] + yr[d, 0]
        else:
            for dx in range(1, 4):
                cps[d, "x", dx].wait_recv()
            panel = stage[d, x] + xr[d, 0, 0] + xr[d, 1, 0] + xr[d, 2, 0]
        j = (z - d) % 8
        pan[d] = panel
        cp = pltpu.make_async_copy(
            pan.at[d], out_hbm.at[:, pl.ds(pl.multiple_of(j * BLK, BLK), BLK)], out_sem.at[d])
        cp.start()
        outs.append(cp)
        if d:
            l2cp[d].wait_recv()
        s = jnp.sum((panel * lift[d]).reshape(8, 8, BLK), axis=0)
        if d:
            sv[d] = s
            vacp[d] = push(sv.at[d], va.at[d], va_s.at[d], va_r.at[d], dev(dz=-d))
        else:
            va[0] = s

    def start(*ds):
        for d in ds:
            sibwait(d)
        rs_start(ds)

    start(0)
    arrive(1, 1)
    arrive(7, 1)
    lift_start()
    arrive(2, 0)
    arrive(6, 0)
    start(1, 7)
    arrive(2, 1)
    arrive(6, 1)
    arrive(3, 0)
    arrive(5, 0)
    start(2, 6)
    rs_mid(0)
    arrive(3, 1)
    arrive(5, 1)
    arrive(4, 0)
    start(3, 5)
    rs_mid(1)
    rs_mid(7)
    arrive(4, 1)
    start(4)
    for cp in l1:
        cp.wait_recv()
    for dz in range(1, 8):
        l2cp[dz] = push(ls1.at[(z + dz) % 8], lift.at[dz], l2_s.at[dz], l2_r.at[dz], dev(dz=dz))
    lift[0] = ls1[z]
    rs_mid(2)
    rs_mid(6)
    rs_mid(3)
    rs_mid(5)
    rs_end(0)
    rs_end(1)
    rs_end(7)
    rs_end(2)
    rs_end(6)
    rs_end(4)
    rs_end(3)
    rs_end(5)

    total = va[0]
    for d in range(1, 8):
        vacp[d].wait_recv()
        total = total + va[d]
    vb_src[...] = total
    vbcp = []
    for i, (dx, dy, dh, dc) in enumerate(plane):
        vbcp.append(push(vb_src, vb.at[i], vb_s.at[i], vb_r.at[i], dev(dx, dy, 0, dh, dc)))
    for cp in vbcp:
        cp.wait_recv()
    total = total + jnp.sum(vb[...], axis=0)
    total = jnp.sum(total, axis=0, keepdims=True)
    own = total[:, 0:32]
    for kk in range(1, 4):
        own = jnp.where(k == kk, total[:, kk * 32:kk * 32 + 32], own)
    var_ref[...] = own
    for cp in outs:
        cp.wait()
    for cp in pending:
        cp.wait_send()


def finish(panel_ref, terms_ref, base_ref, cross_ref, var_ref):
    cross_ref[...] = -panel_ref[...]
    var_ref[...] = base_ref[...] + terms_ref[...]


def per_device(sigma, factor, blk_map, base_var):
    f32 = jnp.float32
    vm = lambda *s: pltpu.VMEM(s, f32)
    dma = lambda n: pltpu.SemaphoreType.DMA((n,))
    vmem = pl.BlockSpec(memory_space=pltpu.VMEM)
    hbm = pl.BlockSpec(memory_space=pl.ANY)
    panel, var = pl.pallas_call(
        kernel,
        out_shape=(jax.ShapeDtypeStruct((64, 1024), f32), jax.ShapeDtypeStruct((1, 32), f32)),
        in_specs=[hbm, hbm, pl.BlockSpec(memory_space=pltpu.SMEM)],
        out_specs=(hbm, vmem),
        scratch_shapes=[
            vm(8, 64, 128), dma(2), dma(8),
            vm(512, 2048), pltpu.VMEM((512, 1536), jnp.bfloat16), vm(8, 128, 512),
            vm(8, 4, 2, 64, 128), vm(8, 3, 2, 64, 128), vm(8, 4, 64, 128), vm(8, 4, 64, 128),
            vm(8, 64, 128), vm(8, 64, 128), vm(8, 64, 128),
            vm(8, 8, 128), vm(8, 8, 128), vm(8, 128), vm(31, 8, 128),
            pltpu.SemaphoreType.DMA,
            dma(16), dma(16), pltpu.SemaphoreType.DMA, pltpu.SemaphoreType.DMA, dma(16), dma(16),
            dma(8), dma(8), dma(8), dma(8),
            dma(24), dma(24), dma(8), dma(8), dma(8), dma(8), dma(31), dma(31),
            vm(7, 64, 128), dma(7), dma(7),
        ],
        compiler_params=pltpu.CompilerParams(
            collective_id=0, has_side_effects=True, vmem_limit_bytes=56 * 2**20
        ),
    )(sigma, factor.T, blk_map)
    cross, var = pl.pallas_call(
        finish,
        out_shape=(jax.ShapeDtypeStruct((64, 1024), f32), jax.ShapeDtypeStruct((1, 32), f32)),
        in_specs=[vmem] * 3,
        out_specs=(vmem, vmem),
    )(panel, var, base_var.reshape(1, 32))
    return cross, var.reshape(32)


def solution(mesh):
    return jax.shard_map(
        per_device,
        mesh=mesh,
        in_specs=(P("col", "row"), P("row", "col"), P("row"), P("col")),
        out_specs=(P(("col", "row"), None), P("col")),
        check_vma=False,
    )
```

```python
import functools

import jax
import jax.numpy as jnp
from jax import lax
from jax.experimental import pallas as pl
from jax.experimental.pallas import tpu as pltpu
from jax.sharding import PartitionSpec as P

MESH = pl.DeviceIdType.MESH
BLK = 128
POS = {0: 0, 4: 1, 1: 2, 7: 3, 2: 4, 6: 5, 3: 6, 5: 7}
XFIRST = (1, 2, 3)


def kernel(
    sig_hbm, fact_hbm, blk_ref, out_hbm, var_ref,
    pan, in_sem, out_sem,
    sig, acat, front, part, xr, yr, stage, ls_src, ls1, lift, sv, va, vb_src, vb,
    sig_sem, agz_s, agz_r, yh_s, yh_r, sib_s, sib_r, l1_s, l1_r, l2_s, l2_r,
    x_s, x_r, y_s, y_r, va_s, va_r, vb_s, vb_r, dr, d_s, d_r,
):
    r = lax.axis_index("row")
    c = lax.axis_index("col")
    x, yl = r // 2, r % 2
    z, yh, co = c // 4, (c // 2) % 2, c % 2
    k = c % 4

    def dev(dx=0, dy=0, dz=0, dh=0, dc=0):
        return (
            ((x + dx) % 4) * 2 + (yl + dy) % 2,
            ((z + dz) % 8) * 4 + ((yh + dh) % 2) * 2 + (co + dc) % 2,
        )

    def send(src, dst, ssem, rsem, to):
        cp = pltpu.make_async_remote_copy(
            src, dst, ssem, rsem, device_id=to, device_id_type=MESH
        )
        cp.start()
        return cp

    pending = []

    def push(*args):
        cp = send(*args)
        pending.append(cp)
        return cp

    everyone = [
        (dx, dy, dh, dc)
        for dx in range(4) for dy in range(2) for dh in range(2) for dc in range(2)
    ]
    plane = everyone[1:]
    barrier = pltpu.get_barrier_semaphore()
    peers = [dev(dx, dy) for dx in range(4) for dy in range(2)][1:]
    peers += [dev(dh=1), dev(dc=1)]
    peers += [dev(dz=dz, dh=dh) for dz in (1, -1) for dh in (0, 1)]
    for to in peers:
        pl.semaphore_signal(barrier, inc=1, device_id=to, device_id_type=MESH)

    def rows(op):
        src_k = k if op == 0 else ((yh + 1) % 2) * 2 + co
        return pl.ds(pl.multiple_of(src_k * 32, 32), 32)

    def piece(d, op):
        return front.at[POS[d], rows(op)]

    cp_fact = pltpu.make_async_copy(fact_hbm, piece(0, 0), in_sem.at[0])
    cp_fact.start()
    cp_sig = pltpu.make_async_copy(sig_hbm, sig, sig_sem)
    cp_sig.start()
    cp_sig.wait()
    def pick(step, carry):
        at = pl.ds(pl.multiple_of(step * 32, 32), 32)
        for i in range(4):
            if i == 3:
                a = sig[at, 15 * BLK:16 * BLK]
            else:
                where = jnp.full((32, BLK), blk_ref[i] - r * 16, jnp.int32)
                a = sig[at, i * BLK:(i + 1) * BLK]
                for b in range(i + 1, i + 13):
                    a = jnp.where(where == b, sig[at, b * BLK:(b + 1) * BLK], a)
            hi = a.astype(jnp.bfloat16)
            lo = (a - hi.astype(jnp.float32)).astype(jnp.bfloat16)
            acat[at, i * BLK:(i + 1) * BLK] = hi
            acat[at, 512 + i * BLK:512 + (i + 1) * BLK] = hi
            acat[at, 1024 + i * BLK:1024 + (i + 1) * BLK] = lo
        return carry

    lax.fori_loop(0, 16, pick, 0)

    pl.semaphore_wait(barrier, len(peers))

    zcp = {}

    def zsend(d, op):
        for side, (dz, nd) in enumerate(((1, d + 1), (-1, (d - 1) % 8))):
            if d != 0 and (side == 0) != (d < 4):
                continue
            if nd == 4 and op != side:
                continue
            slot = nd * 2 + op
            zcp[nd, op] = push(piece(d, op), piece(nd, op), agz_s.at[slot], agz_r.at[slot], dev(dz=dz))

    sibcp = {}

    def sibsend(d, op):
        slot = d * 2 + op
        sibcp[d, op] = push(piece(d, op), piece(d, op), sib_s.at[slot], sib_r.at[slot], dev(dc=1))

    def arrive(d, op):
        zcp[d, op].wait_recv()
        if d != 4:
            zsend(d, op)
        sibsend(d, op)

    cp_fact.wait()
    zsend(0, 0)
    own = piece(0, 0)
    for d, dz in ((1, 1), (7, -1)):
        slot = d * 2 + 1
        zcp[d, 1] = push(own, front.at[POS[d], rows(0)], agz_s.at[slot], agz_r.at[slot], dev(dz=dz, dh=1))
    cp_yh = push(own, own, yh_s, yh_r, dev(dh=1))
    sibsend(0, 0)
    arrive(1, 0)
    arrive(7, 0)
    cp_yh.wait_recv()
    sibsend(0, 1)

    def sibwait(d):
        sibcp[d, 0].wait_recv()
        sibcp[d, 1].wait_recv()

    l1 = []
    l2cp = {}

    def lift_start():
        ft = [front[POS[0], :, i * BLK:(i + 1) * BLK].T for i in range(4)]
        for b in range(4):
            blk = jnp.zeros((BLK, BLK), jnp.float32)
            for i in range(4):
                where = jnp.full((BLK, BLK), blk_ref[i] - r * 16, jnp.int32)
                blk = jnp.where(where == k * 4 + b, ft[i], blk)
            ls_src[2 * b] = blk[:64]
            ls_src[2 * b + 1] = blk[64:]
        for dx in range(4):
            for dy in range(2):
                if dx + dy == 0:
                    continue
                i = dx * 2 + dy
                to = dev(dx, dy)
                l1.append(push(ls_src.at[to[0]], ls1.at[r], l1_s.at[i], l1_r.at[i], to))
        ls1[r] = ls_src[r]

    cps = {}

    def rs_start(ds):
        n = len(ds)
        f = front[POS[ds[0]]:POS[ds[0]] + n].reshape(n * BLK, 512)
        hi = f.astype(jnp.bfloat16)
        lo = (f - hi.astype(jnp.float32)).astype(jnp.bfloat16)
        fcat = jnp.concatenate([hi, lo, hi], axis=1)
        res = lax.dot_general(
            acat[...], fcat, (((1,), (1,)), ((), ())), preferred_element_type=jnp.float32
        )
        for m, d in enumerate(ds):
            part[d] = res[:, m * BLK:(m + 1) * BLK].reshape(4, 2, 64, BLK)
        for d in ds:
            if d == 4:
                for dx in range(4):
                    for dy in range(2):
                        if dx + dy:
                            i = dx * 2 + dy - 1
                            to = dev(dx, dy)
                            cps[d, i] = push(part.at[d, to[0] // 2, to[0] % 2], dr.at[i], d_s.at[i], d_r.at[i], to)
            elif d in XFIRST:
                for dx in range(1, 4):
                    cps[d, "x", dx] = push(
                        part.at[d, (x + dx) % 4], xr.at[d, dx - 1],
                        x_s.at[d * 3 + dx - 1], x_r.at[d * 3 + dx - 1], dev(dx=dx))
            else:
                cps[d, "y"] = push(part.at[d, :, 1 - yl], yr.at[d], y_s.at[d], y_r.at[d], dev(dy=1))

    def rs_mid(d):
        if d in XFIRST:
            for dx in range(1, 4):
                cps[d, "x", dx].wait_recv()
            stage[d, 0:2] = part[d, x] + xr[d, 0] + xr[d, 1] + xr[d, 2]
            cps[d, "y"] = push(stage.at[d, 1 - yl], yr.at[d, 0], y_s.at[d], y_r.at[d], dev(dy=1))
        else:
            cps[d, "y"].wait_recv()
            stage[d] = part[d, :, yl] + yr[d]
            for dx in range(1, 4):
                cps[d, "x", dx] = push(
                    stage.at[d, (x + dx) % 4], xr.at[d, dx - 1, 0],
                    x_s.at[d * 3 + dx - 1], x_r.at[d * 3 + dx - 1], dev(dx=dx))

    vacp = {}
    outs = []

    def rs_end(d):
        if d == 4:
            panel = part[d, x, yl]
            for i in range(7):
                cps[d, i].wait_recv()
                panel = panel + dr[i]
        elif d in XFIRST:
            cps[d, "y"].wait_recv()
            panel = stage[d, yl] + yr[d, 0]
        else:
            for dx in range(1, 4):
                cps[d, "x", dx].wait_recv()
            panel = stage[d, x] + xr[d, 0, 0] + xr[d, 1, 0] + xr[d, 2, 0]
        j = (z - d) % 8
        pan[d] = panel
        cp = pltpu.make_async_copy(
            pan.at[d], out_hbm.at[:, pl.ds(pl.multiple_of(j * BLK, BLK), BLK)], out_sem.at[d])
        cp.start()
        outs.append(cp)
        if d:
            l2cp[d].wait_recv()
        s = jnp.sum((panel * lift[d]).reshape(8, 8, BLK), axis=0)
        if d:
            sv[d] = s
            vacp[d] = push(sv.at[d], va.at[d], va_s.at[d], va_r.at[d], dev(dz=-d))
        else:
            va[0] = s

    def start(*ds):
        for d in ds:
            sibwait(d)
        rs_start(ds)

    start(0)
    arrive(1, 1)
    arrive(7, 1)
    lift_start()
    arrive(2, 0)
    arrive(6, 0)
    start(1, 7)
    arrive(2, 1)
    arrive(6, 1)
    arrive(3, 0)
    arrive(5, 0)
    start(2, 6)
    rs_mid(0)
    arrive(3, 1)
    arrive(5, 1)
    arrive(4, 0)
    start(3, 5)
    rs_mid(1)
    rs_mid(7)
    for cp in l1:
        cp.wait_recv()
    for dz in range(1, 8):
        l2cp[dz] = push(ls1.at[(z + dz) % 8], lift.at[dz], l2_s.at[dz], l2_r.at[dz], dev(dz=dz))
    lift[0] = ls1[z]
    arrive(4, 1)
    start(4)
    rs_mid(2)
    rs_mid(6)
    rs_mid(3)
    rs_mid(5)
    rs_end(0)
    rs_end(1)
    rs_end(7)
    rs_end(2)
    rs_end(6)
    rs_end(4)
    rs_end(3)
    rs_end(5)

    for cp in pending:
        if not any(cp is late for late in vacp.values()):
            cp.wait_send()
    total = va[0]
    for d in range(1, 8):
        vacp[d].wait_recv()
        total = total + va[d]
    vb_src[...] = total
    for i, (dx, dy, dh, dc) in enumerate(plane):
        send(vb_src, vb.at[i], vb_s, vb_r, dev(dx, dy, 0, dh, dc))
    for d in range(1, 8):
        vacp[d].wait_send()
    for cp in outs:
        cp.wait()
    pltpu.make_async_copy(vb, vb, vb_s).wait()
    pltpu.make_async_copy(vb, vb, vb_r).wait()
    total = total + jnp.sum(vb[...], axis=0)
    total = jnp.sum(total, axis=0, keepdims=True)
    own = total[:, 0:32]
    for kk in range(1, 4):
        own = jnp.where(k == kk, total[:, kk * 32:kk * 32 + 32], own)
    var_ref[...] = own


def finish(panel_ref, terms_ref, base_ref, cross_ref, var_ref):
    cross_ref[...] = -panel_ref[...]
    var_ref[...] = base_ref[...] + terms_ref[...]


def per_device(sigma, factor, blk_map, base_var):
    f32 = jnp.float32
    vm = lambda *s: pltpu.VMEM(s, f32)
    dma = lambda n: pltpu.SemaphoreType.DMA((n,))
    vmem = pl.BlockSpec(memory_space=pltpu.VMEM)
    hbm = pl.BlockSpec(memory_space=pl.ANY)
    panel, var = pl.pallas_call(
        kernel,
        out_shape=(jax.ShapeDtypeStruct((64, 1024), f32), jax.ShapeDtypeStruct((1, 32), f32)),
        in_specs=[hbm, hbm, pl.BlockSpec(memory_space=pltpu.SMEM)],
        out_specs=(hbm, vmem),
        scratch_shapes=[
            vm(8, 64, 128), dma(2), dma(8),
            vm(512, 2048), pltpu.VMEM((512, 1536), jnp.bfloat16), vm(8, 128, 512),
            vm(8, 4, 2, 64, 128), vm(8, 3, 2, 64, 128), vm(8, 4, 64, 128), vm(8, 4, 64, 128),
            vm(8, 64, 128), vm(8, 64, 128), vm(8, 64, 128),
            vm(8, 8, 128), vm(8, 8, 128), vm(8, 128), vm(31, 8, 128),
            pltpu.SemaphoreType.DMA,
            dma(16), dma(16), pltpu.SemaphoreType.DMA, pltpu.SemaphoreType.DMA, dma(16), dma(16),
            dma(8), dma(8), dma(8), dma(8),
            dma(24), dma(24), dma(8), dma(8), dma(8), dma(8), pltpu.SemaphoreType.DMA, pltpu.SemaphoreType.DMA,
            vm(7, 64, 128), dma(7), dma(7),
        ],
        compiler_params=pltpu.CompilerParams(
            collective_id=0, has_side_effects=True, vmem_limit_bytes=56 * 2**20
        ),
    )(sigma, factor.T, blk_map)
    cross, var = pl.pallas_call(
        finish,
        out_shape=(jax.ShapeDtypeStruct((64, 1024), f32), jax.ShapeDtypeStruct((1, 32), f32)),
        in_specs=[vmem] * 3,
        out_specs=(vmem, vmem),
    )(panel, var, base_var.reshape(1, 32))
    return cross, var.reshape(32)


def solution(mesh):
    return jax.shard_map(
        per_device,
        mesh=mesh,
        in_specs=(P("col", "row"), P("row", "col"), P("row"), P("col")),
        out_specs=(P(("col", "row"), None), P("col")),
        check_vma=False,
    )
```

```python
import functools

import jax
import jax.numpy as jnp
from jax import lax
from jax.experimental import pallas as pl
from jax.experimental.pallas import tpu as pltpu
from jax.sharding import PartitionSpec as P

MESH = pl.DeviceIdType.MESH
BLK = 128
POS = {0: 0, 4: 1, 1: 2, 7: 3, 2: 4, 6: 5, 3: 6, 5: 7}
XFIRST = (1, 2, 3)


def kernel(
    sig_hbm, fact_hbm, blk_ref, out_hbm, var_ref,
    pan, in_sem, out_sem,
    sig, acat, front, part, xr, yr, stage, ls_src, ls1, lift, sv, va, vb_src, vb,
    sig_sem, agz_s, agz_r, yh_s, yh_r, sib_s, sib_r, l1_s, l1_r, l2_s, l2_r,
    x_s, x_r, y_s, y_r, va_s, va_r, vb_s, vb_r, dr, d_s, d_r,
):
    r = lax.axis_index("row")
    c = lax.axis_index("col")
    x, yl = r // 2, r % 2
    z, yh, co = c // 4, (c // 2) % 2, c % 2
    k = c % 4

    def dev(dx=0, dy=0, dz=0, dh=0, dc=0):
        return (
            ((x + dx) % 4) * 2 + (yl + dy) % 2,
            ((z + dz) % 8) * 4 + ((yh + dh) % 2) * 2 + (co + dc) % 2,
        )

    def send(src, dst, ssem, rsem, to):
        cp = pltpu.make_async_remote_copy(
            src, dst, ssem, rsem, device_id=to, device_id_type=MESH
        )
        cp.start()
        return cp

    pending = []

    def push(*args):
        cp = send(*args)
        pending.append(cp)
        return cp

    everyone = [
        (dx, dy, dh, dc)
        for dx in range(4) for dy in range(2) for dh in range(2) for dc in range(2)
    ]
    plane = everyone[1:]
    barrier = pltpu.get_barrier_semaphore()
    peers = [dev(dx, dy) for dx in range(4) for dy in range(2)][1:]
    peers += [dev(dh=1), dev(dc=1)]
    peers += [dev(dz=dz, dh=dh) for dz in (1, -1) for dh in (0, 1)]
    for to in peers:
        pl.semaphore_signal(barrier, inc=1, device_id=to, device_id_type=MESH)

    def rows(op):
        src_k = k if op == 0 else ((yh + 1) % 2) * 2 + co
        return pl.ds(pl.multiple_of(src_k * 32, 32), 32)

    def piece(d, op):
        return front.at[POS[d], rows(op)]

    cp_fact = pltpu.make_async_copy(fact_hbm, piece(0, 0), in_sem.at[0])
    cp_fact.start()
    cp_sig = pltpu.make_async_copy(sig_hbm, sig, sig_sem)
    cp_sig.start()
    cp_sig.wait()
    def pick(step, carry):
        at = pl.ds(pl.multiple_of(step * 32, 32), 32)
        for i in range(4):
            if i == 3:
                a = sig[at, 15 * BLK:16 * BLK]
            else:
                where = jnp.full((32, BLK), blk_ref[i] - r * 16, jnp.int32)
                a = sig[at, i * BLK:(i + 1) * BLK]
                for b in range(i + 1, i + 13):
                    a = jnp.where(where == b, sig[at, b * BLK:(b + 1) * BLK], a)
            hi = a.astype(jnp.bfloat16)
            lo = (a - hi.astype(jnp.float32)).astype(jnp.bfloat16)
            acat[at, i * BLK:(i + 1) * BLK] = hi
            acat[at, 512 + i * BLK:512 + (i + 1) * BLK] = hi
            acat[at, 1024 + i * BLK:1024 + (i + 1) * BLK] = lo
        return carry

    lax.fori_loop(0, 16, pick, 0)

    pl.semaphore_wait(barrier, len(peers))

    zcp = {}

    def zsend(d, op):
        for side, (dz, nd) in enumerate(((1, d + 1), (-1, (d - 1) % 8))):
            if d != 0 and (side == 0) != (d < 4):
                continue
            if nd == 4 and op != side:
                continue
            slot = nd * 2 + op
            zcp[nd, op] = push(piece(d, op), piece(nd, op), agz_s.at[slot], agz_r.at[slot], dev(dz=dz))

    sibcp = {}

    def sibsend(d, op):
        slot = d * 2 + op
        sibcp[d, op] = push(piece(d, op), piece(d, op), sib_s.at[slot], sib_r.at[slot], dev(dc=1))

    def arrive(d, op):
        zcp[d, op].wait_recv()
        if d != 4:
            zsend(d, op)
        sibsend(d, op)

    cp_fact.wait()
    zsend(0, 0)
    own = piece(0, 0)
    for d, dz in ((1, 1), (7, -1)):
        slot = d * 2 + 1
        zcp[d, 1] = push(own, front.at[POS[d], rows(0)], agz_s.at[slot], agz_r.at[slot], dev(dz=dz, dh=1))
    cp_yh = push(own, own, yh_s, yh_r, dev(dh=1))
    sibsend(0, 0)
    arrive(1, 0)
    arrive(7, 0)
    cp_yh.wait_recv()
    sibsend(0, 1)

    def sibwait(d):
        sibcp[d, 0].wait_recv()
        sibcp[d, 1].wait_recv()

    l1 = []
    l2cp = {}

    def lift_start():
        ft = [front[POS[0], :, i * BLK:(i + 1) * BLK].T for i in range(4)]
        for b in range(4):
            blk = jnp.zeros((BLK, BLK), jnp.float32)
            for i in range(4):
                where = jnp.full((BLK, BLK), blk_ref[i] - r * 16, jnp.int32)
                blk = jnp.where(where == k * 4 + b, ft[i], blk)
            ls_src[2 * b] = blk[:64]
            ls_src[2 * b + 1] = blk[64:]
        for dx in range(4):
            for dy in range(2):
                if dx + dy == 0:
                    continue
                i = dx * 2 + dy
                to = dev(dx, dy)
                l1.append(push(ls_src.at[to[0]], ls1.at[r], l1_s.at[i], l1_r.at[i], to))
        ls1[r] = ls_src[r]

    cps = {}

    def rs_start(ds):
        n = len(ds)
        f = front[POS[ds[0]]:POS[ds[0]] + n].reshape(n * BLK, 512)
        hi = f.astype(jnp.bfloat16)
        lo = (f - hi.astype(jnp.float32)).astype(jnp.bfloat16)
        fcat = jnp.concatenate([hi, lo, hi], axis=1)
        res = lax.dot_general(
            acat[...], fcat, (((1,), (1,)), ((), ())), preferred_element_type=jnp.float32
        )
        for m, d in enumerate(ds):
            part[d] = res[:, m * BLK:(m + 1) * BLK].reshape(4, 2, 64, BLK)
        for d in ds:
            if d == 4:
                for dx in range(4):
                    for dy in range(2):
                        if dx + dy:
                            i = dx * 2 + dy - 1
                            to = dev(dx, dy)
                            cps[d, i] = push(part.at[d, to[0] // 2, to[0] % 2], dr.at[i], d_s.at[i], d_r.at[i], to)
            elif d in XFIRST:
                for dx in range(1, 4):
                    cps[d, "x", dx] = push(
                        part.at[d, (x + dx) % 4], xr.at[d, dx - 1],
                        x_s.at[d * 3 + dx - 1], x_r.at[d * 3 + dx - 1], dev(dx=dx))
            else:
                cps[d, "y"] = push(part.at[d, :, 1 - yl], yr.at[d], y_s.at[d], y_r.at[d], dev(dy=1))

    def rs_mid(d):
        if d in XFIRST:
            for dx in range(1, 4):
                cps[d, "x", dx].wait_recv()
            stage[d, 0:2] = part[d, x] + xr[d, 0] + xr[d, 1] + xr[d, 2]
            cps[d, "y"] = push(stage.at[d, 1 - yl], yr.at[d, 0], y_s.at[d], y_r.at[d], dev(dy=1))
        else:
            cps[d, "y"].wait_recv()
            stage[d] = part[d, :, yl] + yr[d]
            for dx in range(1, 4):
                cps[d, "x", dx] = push(
                    stage.at[d, (x + dx) % 4], xr.at[d, dx - 1, 0],
                    x_s.at[d * 3 + dx - 1], x_r.at[d * 3 + dx - 1], dev(dx=dx))

    vacp = {}
    outs = []

    def rs_end(d):
        if d == 4:
            panel = part[d, x, yl]
            for i in range(7):
                cps[d, i].wait_recv()
                panel = panel + dr[i]
        elif d in XFIRST:
            cps[d, "y"].wait_recv()
            panel = stage[d, yl] + yr[d, 0]
        else:
            for dx in range(1, 4):
                cps[d, "x", dx].wait_recv()
            panel = stage[d, x] + xr[d, 0, 0] + xr[d, 1, 0] + xr[d, 2, 0]
        j = (z - d) % 8
        pan[d] = panel
        cp = pltpu.make_async_copy(
            pan.at[d], out_hbm.at[:, pl.ds(pl.multiple_of(j * BLK, BLK), BLK)], out_sem.at[d])
        cp.start()
        outs.append(cp)
        if d:
            l2cp[d].wait_recv()
        s = jnp.sum((panel * lift[d]).reshape(8, 8, BLK), axis=0).sum(axis=0, keepdims=True)
        if d:
            sv[d] = s
            vacp[d] = push(sv.at[d], va.at[d], va_s.at[d], va_r.at[d], dev(dz=-d))
        else:
            va[0] = s

    def start(*ds):
        for d in ds:
            sibwait(d)
        rs_start(ds)

    start(0)
    arrive(1, 1)
    arrive(7, 1)
    lift_start()
    arrive(2, 0)
    arrive(6, 0)
    start(1, 7)
    arrive(2, 1)
    arrive(6, 1)
    arrive(3, 0)
    arrive(5, 0)
    start(2, 6)
    rs_mid(0)
    arrive(3, 1)
    arrive(5, 1)
    arrive(4, 0)
    start(3, 5)
    rs_mid(1)
    rs_mid(7)
    for cp in l1:
        cp.wait_recv()
    for dz in range(1, 8):
        l2cp[dz] = push(ls1.at[(z + dz) % 8], lift.at[dz], l2_s.at[dz], l2_r.at[dz], dev(dz=dz))
    lift[0] = ls1[z]
    arrive(4, 1)
    start(4)
    rs_mid(2)
    rs_mid(6)
    rs_mid(3)
    rs_mid(5)
    rs_end(0)
    rs_end(1)
    rs_end(7)
    rs_end(2)
    rs_end(6)
    rs_end(4)
    rs_end(3)
    rs_end(5)

    for cp in pending:
        if not any(cp is late for late in vacp.values()):
            cp.wait_send()
    total = va[0]
    for d in range(1, 8):
        vacp[d].wait_recv()
        total = total + va[d]
    vb_src[...] = total
    for i, (dx, dy, dh, dc) in enumerate(plane):
        send(vb_src, vb.at[i], vb_s, vb_r, dev(dx, dy, 0, dh, dc))
    for d in range(1, 8):
        vacp[d].wait_send()
    for cp in outs:
        cp.wait()
    pltpu.make_async_copy(vb, vb, vb_s).wait()
    pltpu.make_async_copy(vb, vb, vb_r).wait()
    total = vb_src[...] + jnp.sum(vb[...], axis=0)
    own = total[:, 0:32]
    for kk in range(1, 4):
        own = jnp.where(k == kk, total[:, kk * 32:kk * 32 + 32], own)
    var_ref[...] = own


def finish(panel_ref, terms_ref, base_ref, cross_ref, var_ref):
    cross_ref[...] = -panel_ref[...]
    var_ref[...] = base_ref[...] + terms_ref[...]


def per_device(sigma, factor, blk_map, base_var):
    f32 = jnp.float32
    vm = lambda *s: pltpu.VMEM(s, f32)
    dma = lambda n: pltpu.SemaphoreType.DMA((n,))
    vmem = pl.BlockSpec(memory_space=pltpu.VMEM)
    hbm = pl.BlockSpec(memory_space=pl.ANY)
    panel, var = pl.pallas_call(
        kernel,
        out_shape=(jax.ShapeDtypeStruct((64, 1024), f32), jax.ShapeDtypeStruct((1, 32), f32)),
        in_specs=[hbm, hbm, pl.BlockSpec(memory_space=pltpu.SMEM)],
        out_specs=(hbm, vmem),
        scratch_shapes=[
            vm(8, 64, 128), dma(2), dma(8),
            vm(512, 2048), pltpu.VMEM((512, 1536), jnp.bfloat16), vm(8, 128, 512),
            vm(8, 4, 2, 64, 128), vm(8, 3, 2, 64, 128), vm(8, 4, 64, 128), vm(8, 4, 64, 128),
            vm(8, 64, 128), vm(8, 64, 128), vm(8, 64, 128),
            vm(8, 1, 128), vm(8, 1, 128), vm(1, 128), vm(31, 1, 128),
            pltpu.SemaphoreType.DMA,
            dma(16), dma(16), pltpu.SemaphoreType.DMA, pltpu.SemaphoreType.DMA, dma(16), dma(16),
            dma(8), dma(8), dma(8), dma(8),
            dma(24), dma(24), dma(8), dma(8), dma(8), dma(8), pltpu.SemaphoreType.DMA, pltpu.SemaphoreType.DMA,
            vm(7, 64, 128), dma(7), dma(7),
        ],
        compiler_params=pltpu.CompilerParams(
            collective_id=0, has_side_effects=True, vmem_limit_bytes=56 * 2**20
        ),
    )(sigma, factor.T, blk_map)
    cross, var = pl.pallas_call(
        finish,
        out_shape=(jax.ShapeDtypeStruct((64, 1024), f32), jax.ShapeDtypeStruct((1, 32), f32)),
        in_specs=[vmem] * 3,
        out_specs=(vmem, vmem),
    )(panel, var, base_var.reshape(1, 32))
    return cross, var.reshape(32)


def solution(mesh):
    return jax.shard_map(
        per_device,
        mesh=mesh,
        in_specs=(P("col", "row"), P("row", "col"), P("row"), P("col")),
        out_specs=(P(("col", "row"), None), P("col")),
        check_vma=False,
    )
```

```python
import functools

import jax
import jax.numpy as jnp
from jax import lax
from jax.experimental import pallas as pl
from jax.experimental.pallas import tpu as pltpu
from jax.sharding import PartitionSpec as P

MESH = pl.DeviceIdType.MESH
BLK = 128
POS = {0: 0, 4: 1, 1: 2, 7: 3, 2: 4, 6: 5, 3: 6, 5: 7}
XFIRST = (1, 2, 3)


def kernel(
    sig_hbm, fact_hbm, blk_ref, out_hbm, var_ref,
    pan, in_sem, out_sem,
    sig, acat, front, part, xr, yr, stage, ls_src, ls1, lift, sv, va, vb_src, vb,
    sig_sem, agz_s, agz_r, yh_s, yh_r, sib_s, sib_r, l1_s, l1_r, l2_s, l2_r,
    x_s, x_r, y_s, y_r, va_s, va_r, vb_s, vb_r, dr, d_s, d_r,
):
    r = lax.axis_index("row")
    c = lax.axis_index("col")
    x, yl = r // 2, r % 2
    z, yh, co = c // 4, (c // 2) % 2, c % 2
    k = c % 4

    def dev(dx=0, dy=0, dz=0, dh=0, dc=0):
        return (
            ((x + dx) % 4) * 2 + (yl + dy) % 2,
            ((z + dz) % 8) * 4 + ((yh + dh) % 2) * 2 + (co + dc) % 2,
        )

    def send(src, dst, ssem, rsem, to):
        cp = pltpu.make_async_remote_copy(
            src, dst, ssem, rsem, device_id=to, device_id_type=MESH
        )
        cp.start()
        return cp

    pending = []

    def push(*args):
        cp = send(*args)
        pending.append(cp)
        return cp

    everyone = [
        (dx, dy, dh, dc)
        for dx in range(4) for dy in range(2) for dh in range(2) for dc in range(2)
    ]
    plane = everyone[1:]
    barrier = pltpu.get_barrier_semaphore()
    peers = [dev(dx, dy) for dx in range(4) for dy in range(2)][1:]
    peers += [dev(dh=1), dev(dc=1)]
    peers += [dev(dz=dz, dh=dh) for dz in (1, -1) for dh in (0, 1)]
    for to in peers:
        pl.semaphore_signal(barrier, inc=1, device_id=to, device_id_type=MESH)

    def rows(op):
        src_k = k if op == 0 else ((yh + 1) % 2) * 2 + co
        return pl.ds(pl.multiple_of(src_k * 32, 32), 32)

    def piece(d, op):
        return front.at[POS[d], rows(op)]

    cp_fact = pltpu.make_async_copy(fact_hbm, piece(0, 0), in_sem.at[0])
    cp_fact.start()
    cp_sig = pltpu.make_async_copy(sig_hbm, sig, sig_sem)
    cp_sig.start()
    cp_sig.wait()
    def pick(step, carry):
        at = pl.ds(pl.multiple_of(step * 32, 32), 32)
        for i in range(4):
            if i == 3:
                a = sig[at, 15 * BLK:16 * BLK]
            else:
                where = jnp.full((32, BLK), blk_ref[i] - r * 16, jnp.int32)
                a = sig[at, i * BLK:(i + 1) * BLK]
                for b in range(i + 1, i + 13):
                    a = jnp.where(where == b, sig[at, b * BLK:(b + 1) * BLK], a)
            hi = a.astype(jnp.bfloat16)
            lo = (a - hi.astype(jnp.float32)).astype(jnp.bfloat16)
            acat[at, i * BLK:(i + 1) * BLK] = hi
            acat[at, 512 + i * BLK:512 + (i + 1) * BLK] = hi
            acat[at, 1024 + i * BLK:1024 + (i + 1) * BLK] = lo
        return carry

    lax.fori_loop(0, 16, pick, 0)

    pl.semaphore_wait(barrier, len(peers))

    zcp = {}

    def zsend(d, op):
        for side, (dz, nd) in enumerate(((1, d + 1), (-1, (d - 1) % 8))):
            if d != 0 and (side == 0) != (d < 4):
                continue
            if nd == 4 and op != side:
                continue
            slot = nd * 2 + op
            zcp[nd, op] = push(piece(d, op), piece(nd, op), agz_s.at[slot], agz_r.at[slot], dev(dz=dz))

    sibcp = {}

    def sibsend(d, op):
        slot = d * 2 + op
        sibcp[d, op] = push(piece(d, op), piece(d, op), sib_s.at[slot], sib_r.at[slot], dev(dc=1))

    def arrive(d, op):
        zcp[d, op].wait_recv()
        if d != 4:
            zsend(d, op)
        sibsend(d, op)

    cp_fact.wait()
    zsend(0, 0)
    own = piece(0, 0)
    for d, dz in ((1, 1), (7, -1)):
        slot = d * 2 + 1
        zcp[d, 1] = push(own, front.at[POS[d], rows(0)], agz_s.at[slot], agz_r.at[slot], dev(dz=dz, dh=1))
    cp_yh = push(own, own, yh_s, yh_r, dev(dh=1))
    sibsend(0, 0)
    arrive(1, 0)
    arrive(7, 0)
    cp_yh.wait_recv()
    sibsend(0, 1)

    def sibwait(d):
        sibcp[d, 0].wait_recv()
        sibcp[d, 1].wait_recv()

    l1 = []
    l2cp = {}

    def lift_start():
        ft = [front[POS[0], :, i * BLK:(i + 1) * BLK].T for i in range(4)]
        for b in range(4):
            blk = jnp.zeros((BLK, BLK), jnp.float32)
            for i in range(4):
                where = jnp.full((BLK, BLK), blk_ref[i] - r * 16, jnp.int32)
                blk = jnp.where(where == k * 4 + b, ft[i], blk)
            ls_src[2 * b] = blk[:64]
            ls_src[2 * b + 1] = blk[64:]
        for dx in range(4):
            for dy in range(2):
                if dx + dy == 0:
                    continue
                i = dx * 2 + dy
                to = dev(dx, dy)
                l1.append(push(ls_src.at[to[0]], ls1.at[r], l1_s.at[i], l1_r.at[i], to))
        ls1[r] = ls_src[r]

    cps = {}

    def rs_start(ds):
        n = len(ds)
        f = front[POS[ds[0]]:POS[ds[0]] + n].reshape(n * BLK, 512)
        hi = f.astype(jnp.bfloat16)
        lo = (f - hi.astype(jnp.float32)).astype(jnp.bfloat16)
        fcat = jnp.concatenate([hi, lo, hi], axis=1)
        res = lax.dot_general(
            acat[...], fcat, (((1,), (1,)), ((), ())), preferred_element_type=jnp.float32
        )
        for m, d in enumerate(ds):
            part[d] = res[:, m * BLK:(m + 1) * BLK].reshape(4, 2, 64, BLK)
        for d in ds:
            if d == 4:
                for dx in range(4):
                    for dy in range(2):
                        if dx + dy:
                            i = dx * 2 + dy - 1
                            to = dev(dx, dy)
                            cps[d, i] = push(part.at[d, to[0] // 2, to[0] % 2], dr.at[i], d_s.at[i], d_r.at[i], to)
            elif d in XFIRST:
                for dx in range(1, 4):
                    cps[d, "x", dx] = push(
                        part.at[d, (x + dx) % 4], xr.at[d, dx - 1],
                        x_s.at[d * 3 + dx - 1], x_r.at[d * 3 + dx - 1], dev(dx=dx))
            else:
                cps[d, "y"] = push(part.at[d, :, 1 - yl], yr.at[d], y_s.at[d], y_r.at[d], dev(dy=1))

    def rs_mid(d):
        if d in XFIRST:
            for dx in range(1, 4):
                cps[d, "x", dx].wait_recv()
            stage[d, 0:2] = part[d, x] + xr[d, 0] + xr[d, 1] + xr[d, 2]
            cps[d, "y"] = push(stage.at[d, 1 - yl], yr.at[d, 0], y_s.at[d], y_r.at[d], dev(dy=1))
        else:
            cps[d, "y"].wait_recv()
            stage[d] = part[d, :, yl] + yr[d]
            for dx in range(1, 4):
                cps[d, "x", dx] = push(
                    stage.at[d, (x + dx) % 4], xr.at[d, dx - 1, 0],
                    x_s.at[d * 3 + dx - 1], x_r.at[d * 3 + dx - 1], dev(dx=dx))

    vacp = {}
    outs = []

    def rs_end(d):
        if d == 4:
            panel = part[d, x, yl]
            for i in range(7):
                cps[d, i].wait_recv()
                panel = panel + dr[i]
        elif d in XFIRST:
            cps[d, "y"].wait_recv()
            panel = stage[d, yl] + yr[d, 0]
        else:
            for dx in range(1, 4):
                cps[d, "x", dx].wait_recv()
            panel = stage[d, x] + xr[d, 0, 0] + xr[d, 1, 0] + xr[d, 2, 0]
        if d:
            l2cp[d].wait_recv()
        s = jnp.sum((panel * lift[d]).reshape(8, 8, BLK), axis=0).sum(axis=0, keepdims=True)
        if d:
            sv[d] = s
            vacp[d] = push(sv.at[d], va.at[d], va_s.at[d], va_r.at[d], dev(dz=-d))
        else:
            va[0] = s
        j = (z - d) % 8
        pan[d] = panel
        cp = pltpu.make_async_copy(
            pan.at[d], out_hbm.at[:, pl.ds(pl.multiple_of(j * BLK, BLK), BLK)], out_sem.at[d])
        cp.start()
        outs.append(cp)

    def start(*ds):
        for d in ds:
            sibwait(d)
        rs_start(ds)

    start(0)
    arrive(1, 1)
    arrive(7, 1)
    lift_start()
    arrive(2, 0)
    arrive(6, 0)
    start(1, 7)
    arrive(2, 1)
    arrive(6, 1)
    arrive(3, 0)
    arrive(5, 0)
    start(2, 6)
    rs_mid(0)
    arrive(3, 1)
    arrive(5, 1)
    arrive(4, 0)
    start(3, 5)
    rs_mid(1)
    rs_mid(7)
    for cp in l1:
        cp.wait_recv()
    for dz in range(1, 8):
        l2cp[dz] = push(ls1.at[(z + dz) % 8], lift.at[dz], l2_s.at[dz], l2_r.at[dz], dev(dz=dz))
    lift[0] = ls1[z]
    arrive(4, 1)
    start(4)
    rs_mid(2)
    rs_mid(6)
    rs_end(0)
    rs_end(1)
    rs_end(7)
    rs_mid(3)
    rs_mid(5)
    rs_end(2)
    rs_end(6)
    rs_end(4)
    rs_end(3)
    rs_end(5)

    for cp in pending:
        if not any(cp is late for late in vacp.values()):
            cp.wait_send()
    total = va[0]
    for d in range(1, 8):
        vacp[d].wait_recv()
        total = total + va[d]
    vb_src[...] = total
    for i, (dx, dy, dh, dc) in enumerate(plane):
        send(vb_src, vb.at[i], vb_s, vb_r, dev(dx, dy, 0, dh, dc))
    for d in range(1, 8):
        vacp[d].wait_send()
    for cp in outs:
        cp.wait()
    pltpu.make_async_copy(vb, vb, vb_s).wait()
    pltpu.make_async_copy(vb, vb, vb_r).wait()
    total = vb_src[...] + jnp.sum(vb[...], axis=0)
    own = total[:, 0:32]
    for kk in range(1, 4):
        own = jnp.where(k == kk, total[:, kk * 32:kk * 32 + 32], own)
    var_ref[...] = own


def finish(panel_ref, terms_ref, base_ref, cross_ref, var_ref):
    cross_ref[...] = -panel_ref[...]
    var_ref[...] = base_ref[...] + terms_ref[...]


def per_device(sigma, factor, blk_map, base_var):
    f32 = jnp.float32
    vm = lambda *s: pltpu.VMEM(s, f32)
    dma = lambda n: pltpu.SemaphoreType.DMA((n,))
    vmem = pl.BlockSpec(memory_space=pltpu.VMEM)
    hbm = pl.BlockSpec(memory_space=pl.ANY)
    panel, var = pl.pallas_call(
        kernel,
        out_shape=(jax.ShapeDtypeStruct((64, 1024), f32), jax.ShapeDtypeStruct((1, 32), f32)),
        in_specs=[hbm, hbm, pl.BlockSpec(memory_space=pltpu.SMEM)],
        out_specs=(hbm, vmem),
        scratch_shapes=[
            vm(8, 64, 128), dma(2), dma(8),
            vm(512, 2048), pltpu.VMEM((512, 1536), jnp.bfloat16), vm(8, 128, 512),
            vm(8, 4, 2, 64, 128), vm(8, 3, 2, 64, 128), vm(8, 4, 64, 128), vm(8, 4, 64, 128),
            vm(8, 64, 128), vm(8, 64, 128), vm(8, 64, 128),
            vm(8, 1, 128), vm(8, 1, 128), vm(1, 128), vm(31, 1, 128),
            pltpu.SemaphoreType.DMA,
            dma(16), dma(16), pltpu.SemaphoreType.DMA, pltpu.SemaphoreType.DMA, dma(16), dma(16),
            dma(8), dma(8), dma(8), dma(8),
            dma(24), dma(24), dma(8), dma(8), dma(8), dma(8), pltpu.SemaphoreType.DMA, pltpu.SemaphoreType.DMA,
            vm(7, 64, 128), dma(7), dma(7),
        ],
        compiler_params=pltpu.CompilerParams(
            collective_id=0, has_side_effects=True, vmem_limit_bytes=56 * 2**20
        ),
    )(sigma, factor.T, blk_map)
    cross, var = pl.pallas_call(
        finish,
        out_shape=(jax.ShapeDtypeStruct((64, 1024), f32), jax.ShapeDtypeStruct((1, 32), f32)),
        in_specs=[vmem] * 3,
        out_specs=(vmem, vmem),
    )(panel, var, base_var.reshape(1, 32))
    return cross, var.reshape(32)


def solution(mesh):
    return jax.shard_map(
        per_device,
        mesh=mesh,
        in_specs=(P("col", "row"), P("row", "col"), P("row"), P("col")),
        out_specs=(P(("col", "row"), None), P("col")),
        check_vma=False,
    )
```

```python
import functools

import jax
import jax.numpy as jnp
from jax import lax
from jax.experimental import pallas as pl
from jax.experimental.pallas import tpu as pltpu
from jax.sharding import PartitionSpec as P

MESH = pl.DeviceIdType.MESH
BLK = 128
POS = {0: 0, 4: 1, 1: 2, 7: 3, 2: 4, 6: 5, 3: 6, 5: 7}
XFIRST = (1, 2, 3)


def kernel(
    sig_hbm, fact_hbm, blk_ref, out_hbm, var_ref,
    pan, in_sem, out_sem,
    sig, acat, front, part, xr, yr, stage, ls_src, ls1, lift, sv, va, vb_src, vb,
    sig_sem, agz_s, agz_r, yh_s, yh_r, sib_s, sib_r, l1_s, l1_r, l2_s, l2_r,
    x_s, x_r, y_s, y_r, va_s, va_r, vb_s, vb_r, dr, d_s, d_r,
):
    r = lax.axis_index("row")
    c = lax.axis_index("col")
    x, yl = r // 2, r % 2
    z, yh, co = c // 4, (c // 2) % 2, c % 2
    k = c % 4

    def dev(dx=0, dy=0, dz=0, dh=0, dc=0):
        return (
            ((x + dx) % 4) * 2 + (yl + dy) % 2,
            ((z + dz) % 8) * 4 + ((yh + dh) % 2) * 2 + (co + dc) % 2,
        )

    def send(src, dst, ssem, rsem, to):
        cp = pltpu.make_async_remote_copy(
            src, dst, ssem, rsem, device_id=to, device_id_type=MESH
        )
        cp.start()
        return cp

    def drain(ref, sem):
        pltpu.make_async_copy(ref, ref, sem).wait()

    pending = []

    def push(*args):
        cp = send(*args)
        pending.append(cp)
        return cp

    everyone = [
        (dx, dy, dh, dc)
        for dx in range(4) for dy in range(2) for dh in range(2) for dc in range(2)
    ]
    plane = everyone[1:]
    barrier = pltpu.get_barrier_semaphore()
    peers = [dev(dx, dy) for dx in range(4) for dy in range(2)][1:]
    peers += [dev(dh=1), dev(dc=1)]
    peers += [dev(dz=dz, dh=dh) for dz in (1, -1) for dh in (0, 1)]
    for to in peers:
        pl.semaphore_signal(barrier, inc=1, device_id=to, device_id_type=MESH)

    def rows(op):
        src_k = k if op == 0 else ((yh + 1) % 2) * 2 + co
        return pl.ds(pl.multiple_of(src_k * 32, 32), 32)

    def piece(d, op):
        return front.at[POS[d], rows(op)]

    cp_fact = pltpu.make_async_copy(fact_hbm, piece(0, 0), in_sem.at[0])
    cp_fact.start()
    cp_sig = pltpu.make_async_copy(sig_hbm, sig, sig_sem)
    cp_sig.start()
    cp_sig.wait()
    def pick(step, carry):
        at = pl.ds(pl.multiple_of(step * 32, 32), 32)
        for i in range(4):
            if i == 3:
                a = sig[at, 15 * BLK:16 * BLK]
            else:
                where = jnp.full((32, BLK), blk_ref[i] - r * 16, jnp.int32)
                a = sig[at, i * BLK:(i + 1) * BLK]
                for b in range(i + 1, i + 13):
                    a = jnp.where(where == b, sig[at, b * BLK:(b + 1) * BLK], a)
            hi = a.astype(jnp.bfloat16)
            lo = (a - hi.astype(jnp.float32)).astype(jnp.bfloat16)
            acat[at, i * BLK:(i + 1) * BLK] = hi
            acat[at, 512 + i * BLK:512 + (i + 1) * BLK] = hi
            acat[at, 1024 + i * BLK:1024 + (i + 1) * BLK] = lo
        return carry

    lax.fori_loop(0, 16, pick, 0)

    pl.semaphore_wait(barrier, len(peers))

    zcp = {}

    def zsend(d, op):
        for side, (dz, nd) in enumerate(((1, d + 1), (-1, (d - 1) % 8))):
            if d != 0 and (side == 0) != (d < 4):
                continue
            if nd == 4 and op != side:
                continue
            slot = nd * 2 + op
            zcp[nd, op] = push(piece(d, op), piece(nd, op), agz_s.at[slot], agz_r.at[slot], dev(dz=dz))

    sibcp = {}

    def sibsend(d, op):
        slot = d * 2 + op
        sibcp[d, op] = push(piece(d, op), piece(d, op), sib_s.at[slot], sib_r.at[d], dev(dc=1))

    def arrive(d, op):
        zcp[d, op].wait_recv()
        if d != 4:
            zsend(d, op)
        sibsend(d, op)

    cp_fact.wait()
    zsend(0, 0)
    own = piece(0, 0)
    for d, dz in ((1, 1), (7, -1)):
        slot = d * 2 + 1
        zcp[d, 1] = push(own, front.at[POS[d], rows(0)], agz_s.at[slot], agz_r.at[slot], dev(dz=dz, dh=1))
    cp_yh = push(own, own, yh_s, yh_r, dev(dh=1))
    sibsend(0, 0)
    arrive(1, 0)
    arrive(7, 0)
    cp_yh.wait_recv()
    sibsend(0, 1)

    def sibwait(d):
        drain(front.at[POS[d], 0:64], sib_r.at[d])

    l1 = []
    l2cp = {}

    def lift_start():
        ft = [front[POS[0], :, i * BLK:(i + 1) * BLK].T for i in range(4)]
        for b in range(4):
            blk = jnp.zeros((BLK, BLK), jnp.float32)
            for i in range(4):
                where = jnp.full((BLK, BLK), blk_ref[i] - r * 16, jnp.int32)
                blk = jnp.where(where == k * 4 + b, ft[i], blk)
            ls_src[2 * b] = blk[:64]
            ls_src[2 * b + 1] = blk[64:]
        for dx in range(4):
            for dy in range(2):
                if dx + dy == 0:
                    continue
                i = dx * 2 + dy
                to = dev(dx, dy)
                l1.append(push(ls_src.at[to[0]], ls1.at[r], l1_s.at[i], l1_r.at[i], to))
        ls1[r] = ls_src[r]

    cps = {}

    def rs_start(ds):
        n = len(ds)
        f = front[POS[ds[0]]:POS[ds[0]] + n].reshape(n * BLK, 512)
        hi = f.astype(jnp.bfloat16)
        lo = (f - hi.astype(jnp.float32)).astype(jnp.bfloat16)
        fcat = jnp.concatenate([hi, lo, hi], axis=1)
        res = lax.dot_general(
            acat[...], fcat, (((1,), (1,)), ((), ())), preferred_element_type=jnp.float32
        )
        for m, d in enumerate(ds):
            part[d] = res[:, m * BLK:(m + 1) * BLK].reshape(4, 2, 64, BLK)
        for d in ds:
            if d == 4:
                for dx in range(4):
                    for dy in range(2):
                        if dx + dy:
                            i = dx * 2 + dy - 1
                            to = dev(dx, dy)
                            cps[d, i] = push(part.at[d, to[0] // 2, to[0] % 2], dr.at[i], d_s.at[i], d_r.at[0], to)
            elif d in XFIRST:
                for dx in range(1, 4):
                    cps[d, "x", dx] = push(
                        part.at[d, (x + dx) % 4], xr.at[d, dx - 1],
                        x_s.at[d * 3 + dx - 1], x_r.at[d], dev(dx=dx))
            else:
                cps[d, "y"] = push(part.at[d, :, 1 - yl], yr.at[d], y_s.at[d], y_r.at[d], dev(dy=1))

    def rs_mid(d):
        if d in XFIRST:
            drain(xr.at[d], x_r.at[d])
            stage[d, 0:2] = part[d, x] + xr[d, 0] + xr[d, 1] + xr[d, 2]
            cps[d, "y"] = push(stage.at[d, 1 - yl], yr.at[d, 0], y_s.at[d], y_r.at[d], dev(dy=1))
        else:
            cps[d, "y"].wait_recv()
            stage[d] = part[d, :, yl] + yr[d]
            for dx in range(1, 4):
                cps[d, "x", dx] = push(
                    stage.at[d, (x + dx) % 4], xr.at[d, dx - 1, 0],
                    x_s.at[d * 3 + dx - 1], x_r.at[d], dev(dx=dx))

    vacp = {}
    outs = []

    def rs_end(d):
        if d == 4:
            panel = part[d, x, yl]
            drain(dr, d_r.at[0])
            for i in range(7):
                panel = panel + dr[i]
        elif d in XFIRST:
            cps[d, "y"].wait_recv()
            panel = stage[d, yl] + yr[d, 0]
        else:
            drain(xr.at[d, :, 0], x_r.at[d])
            panel = stage[d, x] + xr[d, 0, 0] + xr[d, 1, 0] + xr[d, 2, 0]
        if d:
            l2cp[d].wait_recv()
        s = jnp.sum((panel * lift[d]).reshape(8, 8, BLK), axis=0).sum(axis=0, keepdims=True)
        if d:
            sv[d] = s
            vacp[d] = push(sv.at[d], va.at[d], va_s.at[d], va_r.at[0], dev(dz=-d))
        else:
            va[0] = s
        j = (z - d) % 8
        pan[d] = panel
        cp = pltpu.make_async_copy(
            pan.at[d], out_hbm.at[:, pl.ds(pl.multiple_of(j * BLK, BLK), BLK)], out_sem.at[d])
        cp.start()
        outs.append(cp)

    def start(*ds):
        for d in ds:
            sibwait(d)
        rs_start(ds)

    start(0)
    arrive(1, 1)
    arrive(7, 1)
    lift_start()
    arrive(2, 0)
    arrive(6, 0)
    start(1, 7)
    arrive(2, 1)
    arrive(6, 1)
    arrive(3, 0)
    arrive(5, 0)
    start(2, 6)
    rs_mid(0)
    arrive(3, 1)
    arrive(5, 1)
    arrive(4, 0)
    start(3, 5)
    rs_mid(1)
    rs_mid(7)
    for cp in l1:
        cp.wait_recv()
    for dz in range(1, 8):
        l2cp[dz] = push(ls1.at[(z + dz) % 8], lift.at[dz], l2_s.at[dz], l2_r.at[dz], dev(dz=dz))
    lift[0] = ls1[z]
    arrive(4, 1)
    start(4)
    rs_mid(2)
    rs_mid(6)
    rs_end(0)
    rs_end(1)
    rs_end(7)
    rs_mid(3)
    rs_mid(5)
    rs_end(2)
    rs_end(6)
    rs_end(4)
    rs_end(3)
    rs_end(5)

    for cp in pending:
        if not any(cp is late for late in vacp.values()):
            cp.wait_send()
    total = va[0]
    drain(va.at[1:8], va_r.at[0])
    for d in range(1, 8):
        total = total + va[d]
    vb_src[...] = total
    for i, (dx, dy, dh, dc) in enumerate(plane):
        send(vb_src, vb.at[i], vb_s, vb_r, dev(dx, dy, 0, dh, dc))
    for d in range(1, 8):
        vacp[d].wait_send()
    for cp in outs:
        cp.wait()
    pltpu.make_async_copy(vb, vb, vb_s).wait()
    pltpu.make_async_copy(vb, vb, vb_r).wait()
    total = vb_src[...] + jnp.sum(vb[...], axis=0)
    own = total[:, 0:32]
    for kk in range(1, 4):
        own = jnp.where(k == kk, total[:, kk * 32:kk * 32 + 32], own)
    var_ref[...] = own


def finish(panel_ref, terms_ref, base_ref, cross_ref, var_ref):
    cross_ref[...] = -panel_ref[...]
    var_ref[...] = base_ref[...] + terms_ref[...]


def per_device(sigma, factor, blk_map, base_var):
    f32 = jnp.float32
    vm = lambda *s: pltpu.VMEM(s, f32)
    dma = lambda n: pltpu.SemaphoreType.DMA((n,))
    vmem = pl.BlockSpec(memory_space=pltpu.VMEM)
    hbm = pl.BlockSpec(memory_space=pl.ANY)
    panel, var = pl.pallas_call(
        kernel,
        out_shape=(jax.ShapeDtypeStruct((64, 1024), f32), jax.ShapeDtypeStruct((1, 32), f32)),
        in_specs=[hbm, hbm, pl.BlockSpec(memory_space=pltpu.SMEM)],
        out_specs=(hbm, vmem),
        scratch_shapes=[
            vm(8, 64, 128), dma(2), dma(8),
            vm(512, 2048), pltpu.VMEM((512, 1536), jnp.bfloat16), vm(8, 128, 512),
            vm(8, 4, 2, 64, 128), vm(8, 3, 2, 64, 128), vm(8, 4, 64, 128), vm(8, 4, 64, 128),
            vm(8, 64, 128), vm(8, 64, 128), vm(8, 64, 128),
            vm(8, 1, 128), vm(8, 1, 128), vm(1, 128), vm(31, 1, 128),
            pltpu.SemaphoreType.DMA,
            dma(16), dma(16), pltpu.SemaphoreType.DMA, pltpu.SemaphoreType.DMA, dma(16), dma(16),
            dma(8), dma(8), dma(8), dma(8),
            dma(24), dma(24), dma(8), dma(8), dma(8), dma(8), pltpu.SemaphoreType.DMA, pltpu.SemaphoreType.DMA,
            vm(7, 64, 128), dma(7), dma(7),
        ],
        compiler_params=pltpu.CompilerParams(
            collective_id=0, has_side_effects=True, vmem_limit_bytes=56 * 2**20
        ),
    )(sigma, factor.T, blk_map)
    cross, var = pl.pallas_call(
        finish,
        out_shape=(jax.ShapeDtypeStruct((64, 1024), f32), jax.ShapeDtypeStruct((1, 32), f32)),
        in_specs=[vmem] * 3,
        out_specs=(vmem, vmem),
    )(panel, var, base_var.reshape(1, 32))
    return cross, var.reshape(32)


def solution(mesh):
    return jax.shard_map(
        per_device,
        mesh=mesh,
        in_specs=(P("col", "row"), P("row", "col"), P("row"), P("col")),
        out_specs=(P(("col", "row"), None), P("col")),
        check_vma=False,
    )
```
